256 devices in a mesh: grp: 8 (over z_hi, x), dev: 32 (over z_lo, y, core).
Axes of the slice: x: 4, y: 4, z: 8 (z_hi: 2, z_lo: 4; z = z_hi * 4 + z_lo), core: 2. Of those that a mesh axis runs over, the one named last changes fastest.
Arguments:
- sources: bfloat16 [2048, 2, 256, 512], P(('grp', 'dev')), may hold values from -6 to 6
- leaf_in: bfloat16 [2048, 64, 512], P(('grp', 'dev')), may hold values from -0.25 to 0.25
- own_blocks: bfloat16 [11, 2048, 64, 128], P(None, ('grp', 'dev')), may hold values from -0.375 to 0.375
- cross_blocks: bfloat16 [11, 2048, 64, 128], P(None, ('grp', 'dev')), may hold values from -0.375 to 0.375
- leaf_out: bfloat16 [2048, 256, 128], P(('grp', 'dev')), may hold values from -0.5 to 0.5
Outputs:
- potentials: bfloat16 [2048, 2, 256, 512], P(('grp', 'dev'))
The draws below stay inside these ranges and needn't reach their ends.
All inputs are finite; a program needn't handle non-finite values.
Results may differ from the reference program's by a relative error of at most 0.03.
Values may be sent and summed in bfloat16 or wider, within the bound.
A program may use at most 64 MiB of HBM per device.

```python
import jax
import jax.numpy as jnp

RANK = 64
LEAF = 256
NRHS = 512
LEVELS = 11
NODES = 2048


def block_levels(rng, extent, split, smallest, top_value):
    loudness = 1.0
    for position, blocks in split:
        draws = jax.random.uniform(jax.random.fold_in(jax.random.fold_in(rng, 6), position), (blocks,), jnp.float32, smallest / len(split), top_value / len(split))
        loudness = loudness * jnp.repeat(jnp.exp(draws), extent[position] // blocks).reshape((-1,) + (1,) * (len(extent) - 1 - position))
    return loudness


def bell_draw(own_key, extent, deviation, bound, shards=(), kind=jnp.bfloat16):
    level = block_levels(own_key, extent, shards, -0.22, 0.18) if shards else 1.0
    array = jax.random.normal(own_key, extent, jnp.float32) * deviation * level
    return jnp.minimum(jnp.maximum(array, -bound), bound).astype(kind)


def setup_inputs(seed: int = 0) -> dict:
    key_of = jax.random.split(jax.random.key(seed), 6)
    sources = bell_draw(key_of[0], (NODES, 2, LEAF, NRHS), 1.0, 6.0, ((0, 256),))
    leaf_in = bell_draw(key_of[1], (NODES, RANK, 2 * LEAF), (2 * LEAF) ** -0.5, 0.25, ((0, 256),))
    own_blocks = bell_draw(key_of[2], (LEVELS, NODES, RANK, 2 * RANK), (4 * RANK) ** -0.5, 0.375, ((1, 256),))
    cross_blocks = bell_draw(key_of[3], (LEVELS, NODES, RANK, 2 * RANK), (4 * RANK) ** -0.5, 0.375, ((1, 256),))
    leaf_out = bell_draw(key_of[4], (NODES, LEAF, 2 * RANK), (2 * RANK) ** -0.5, 0.5, ((0, 256),))
    return dict(sources=sources, leaf_in=leaf_in, own_blocks=own_blocks, cross_blocks=cross_blocks, leaf_out=leaf_out)


def realify(blocks, half):
    real_part = blocks[..., :half]
    imag_part = blocks[..., half:]
    upper = jnp.concatenate([real_part, -imag_part], -1)
    lower = jnp.concatenate([imag_part, real_part], -1)
    return jnp.concatenate([upper, lower], -2)


def apply_blocks(blocks, values):
    return jnp.einsum("nij,njk->nik", blocks.astype(jnp.float32), values.astype(jnp.float32))


def partner(values, stride):
    count = values.shape[0]
    shaped = values.reshape((count // (2 * stride), 2, stride) + values.shape[1:])
    return shaped[:, ::-1].reshape(values.shape)


def reference(sources, leaf_in, own_blocks, cross_blocks, leaf_out):
    count = sources.shape[0]
    flat = sources.reshape(count, 2 * LEAF, NRHS)
    coef = apply_blocks(realify(leaf_in, LEAF), flat).astype(jnp.bfloat16)
    for level in range(LEVELS):
        mine = apply_blocks(realify(own_blocks[level], RANK), coef)
        term = apply_blocks(realify(cross_blocks[level], RANK), coef).astype(jnp.bfloat16)
        coef = (mine + partner(term, 2 ** level).astype(jnp.float32)).astype(jnp.bfloat16)
    result = apply_blocks(realify(leaf_out, RANK), coef).astype(jnp.bfloat16)
    return result.reshape(count, 2, LEAF, NRHS)
```

```python
import functools

import jax
import jax.numpy as jnp
from jax import lax
from jax.experimental import pallas as pl
from jax.experimental.pallas import tpu as pltpu
from jax.sharding import PartitionSpec as P

RANK = 64
LEAF = 256
COLUMNS = 512
CHUNKS = 2
WIDTH = COLUMNS // CHUNKS
LEVELS = 11
MESH = pl.DeviceIdType.MESH
F32 = jnp.float32
BF16 = jnp.bfloat16


def div(a, b):
    return a // b if isinstance(a, int) else lax.div(a, jnp.int32(b))


def rem(a, b):
    return a % b if isinstance(a, int) else lax.rem(a, jnp.int32(b))


def xor(a, b, bits):
    total = 0
    for bit in range(bits):
        one, two = rem(div(a, 2**bit), 2), rem(div(b, 2**bit), 2)
        total = total + rem(one + two, 2) * 2**bit
    return total


def device(x, y, z, core):
    return {"grp": div(z, 4) * 4 + x, "dev": rem(z, 4) * 8 + y * 2 + core}


def realify(block, half):
    real_part, imag_part = block[:, :half], block[:, half:]
    upper = jnp.concatenate([real_part, -imag_part], 1)
    lower = jnp.concatenate([imag_part, real_part], 1)
    return jnp.concatenate([upper, lower], 0)


def pairs(bit):
    step = 2**bit
    return [(s, s + step) for s in range(8) if not s & step]


def butterfly(
    sources, leaf_in, own, cross, out,
    src, leaf, w_loc, w_core, w_y, w_z, w_x, big,
    a_buf, b_buf, core_buf, y_send, y_buf, z_send, z_buf, x_send, x_buf, r_send,
    load_sem, wc_s, wc_r, wy_s, wy_r, wz_s, wz_r, wx_s, wx_r,
    c_s, c_r, y_s, y_r, z_s, z_r, x_s, x_r, r_s, r_r,
):
    grp, dev = lax.axis_index("grp"), lax.axis_index("dev")
    x, y, z = rem(grp, 4), rem(div(dev, 2), 4), div(grp, 4) * 4 + div(dev, 8)
    core = rem(dev, 2)
    z_lo, z_hi = rem(z, 4), div(z, 4)
    sent = []

    def send(from_ref, to_ref, send_sem, recv_sem, target, here=None):
        copy = pltpu.make_async_remote_copy(
            src_ref=from_ref, dst_ref=to_ref, send_sem=send_sem, recv_sem=recv_sem,
            device_id=target, device_id_type=MESH,
        )
        if here is None:
            copy.start()
        else:
            pl.when(here)(pltpu.make_async_copy(from_ref, to_ref, recv_sem).start)
            pl.when(jnp.logical_not(here))(copy.start)
        sent.append((copy, here))

    def keep(from_ref, to_ref, sem):
        pltpu.make_async_copy(from_ref, to_ref, sem).start()

    def arrived(ref, sem):
        pltpu.make_async_copy(ref, ref, sem).wait()

    kinds = (own, cross)
    loads = [pltpu.make_async_copy(leaf_in, leaf, load_sem.at[0])]
    for kind in range(2):
        loads.append(pltpu.make_async_copy(kinds[kind].at[pl.ds(0, 4)], w_loc.at[kind], load_sem.at[1 + kind]))
    for k in range(8):
        loads.append(pltpu.make_async_copy(sources.at[k], src.at[k], load_sem.at[3 + k]))
    for copy in loads:
        copy.start()

    barrier = pltpu.get_barrier_semaphore()

    def greet(target, here=None):
        def signal():
            pl.semaphore_signal(barrier, inc=1, device_id=target, device_id_type=MESH)

        if here is None:
            signal()
        else:
            pl.when(jnp.logical_not(here))(signal)

    greet(device(x, y, z, 1 - core))
    for i in range(1, 4):
        greet(device(x, xor(y, i, 2), z, core))
        greet(device(xor(x, i, 2), y, z, core))
    for m in range(1, 8):
        greet(device(x, y, xor(z, m, 3), core))
    for m in range(8):
        here = None if m else z_lo == 0
        greet(device(x, xor(y, z_lo, 2), xor(z, m, 3), core), here)
        offset = x + 4 * (m // 4)
        here = (x == 0) if m == 0 else None
        greet(device(xor(x, m % 4, 2) , y, xor(z, offset, 3), core), here)
        i, h = m % 4, m // 4
        from_x = xor(x, i, 2)
        greet(device(from_x, y, xor(z_lo, from_x, 2) + 4 * xor(z_hi, h, 1), core), here)
    absent = jnp.where(z_lo == 0, 1, 0) + jnp.where(x == 0, 2, 0)
    count = 1 + 6 + 7 + 24 - absent

    def assemble(level, bit, w, at, p_range=range(4)):
        for p in p_range:
            s, t = pairs(bit)[p]
            def block(kind, k):
                return realify(w[kind, at, k // 4, k % 4], RANK)
            big[level, p] = jnp.concatenate(
                [
                    jnp.concatenate([block(0, s), block(1, t)], 1),
                    jnp.concatenate([block(1, s), block(0, t)], 1),
                ],
                0,
            )

    loads[1].wait()
    loads[2].wait()
    for level in range(3):
        assemble(level, level, w_loc, level)

    pl.semaphore_wait(barrier, count)

    send(cross.at[3], w_core, wc_s.at[0], wc_r.at[0], device(x, y, z, 1 - core))
    for i in range(4):
        t = xor(y, i, 2)
        for kind in range(2):
            refs = (kinds[kind].at[pl.ds(4, 2), :, t], w_y.at[kind, :, :, y])
            if i:
                send(*refs, wy_s.at[kind, i], wy_r.at[kind, y], device(x, t, z, core))
            else:
                keep(*refs, wy_r.at[kind, y])
    for m in range(8):
        q = xor(z, m, 3)
        slot, c = xor(rem(q, 4), y, 2), div(q, 4)
        for kind in range(2):
            refs = (kinds[kind].at[pl.ds(6, 2), c, slot], w_z.at[kind, :, z_hi, z_lo])
            if m:
                send(*refs, wz_s.at[kind, m], wz_r.at[kind, z], device(x, y, q, core))
            else:
                keep(*refs, wz_r.at[kind, z])
    for m in range(8):
        q = xor(z, m, 3)
        slot, c = xor(rem(q, 4), y, 2), div(q, 4)
        for kind in range(2):
            send(
                kinds[kind].at[pl.ds(8, 3), c, slot], w_x.at[kind, :, z_hi, x],
                wx_s.at[kind, m], wx_r.at[kind, x + 4 * z_hi],
                device(m % 4, y, q, core), None if m else x == 0,
            )

    loads[0].wait()
    for k in range(8):
        loads[3 + k].wait()
        value = jnp.dot(realify(leaf[k], LEAF), src[k], preferred_element_type=F32).astype(BF16)
        for ch in range(CHUNKS):
            a_buf[ch, k // 4, k % 4] = value[:, ch * WIDTH : (ch + 1) * WIDTH]

    def step(level, bit, source, target, ch_s, ch_t):
        for p, (s, t) in enumerate(pairs(bit)):
            stacked = jnp.concatenate([source[ch_s, s // 4, s % 4], source[ch_s, t // 4, t % 4]], 0)
            value = jnp.dot(big[level, p], stacked, preferred_element_type=F32).astype(BF16)
            target[ch_t, s // 4, s % 4] = value[:128]
            target[ch_t, t // 4, t % 4] = value[128:]

    for ch in range(CHUNKS):
        step(0, 0, a_buf, b_buf, ch, 0)
        step(1, 1, b_buf, b_buf, 0, 1)
        step(2, 2, b_buf, a_buf, 1, ch)
        send(a_buf.at[ch], core_buf.at[ch], c_s.at[ch], c_r.at[ch], device(x, y, z, 1 - core))

    arrived(w_core, wc_r.at[0])
    for k in range(8):
        big[3, k // 2, pl.ds(128 * (k % 2), 128)] = jnp.concatenate(
            [realify(w_loc[0, 3, k // 4, k % 4], RANK), realify(w_core[k // 4, k % 4], RANK)], 1
        )
    for ch in range(CHUNKS):
        arrived(core_buf.at[ch], c_r.at[ch])
        for k in range(8):
            stacked = jnp.concatenate([a_buf[ch, k // 4, k % 4], core_buf[ch, k // 4, k % 4]], 0)
            y_send[ch, k // 4, k % 4] = jnp.dot(
                big[3, k // 2, pl.ds(128 * (k % 2), 128)], stacked, preferred_element_type=F32
            ).astype(BF16)
        for i in range(4):
            t = xor(y, i, 2)
            refs = (y_send.at[ch, :, t], y_buf.at[ch, :, y])
            if i:
                send(*refs, y_s.at[ch, i], y_r.at[ch, y], device(x, t, z, core))
            else:
                keep(*refs, y_r.at[ch, y])

    for kind in range(2):
        for t in range(4):
            arrived(w_y.at[kind, :, :, t], wy_r.at[kind, t])
    for level in (4, 5):
        assemble(level, level - 4, w_y, level - 4)
    for ch in range(CHUNKS):
        for t in range(4):
            arrived(y_buf.at[ch, :, t], y_r.at[ch, t])
        step(4, 0, y_buf, b_buf, ch, 0)
        step(5, 1, b_buf, z_send, 0, ch)
        for m in range(8):
            q = xor(z, m, 3)
            t, c = xor(y, rem(q, 4), 2), div(q, 4)
            send(
                z_send.at[ch, c, t], z_buf.at[ch, z_hi, z_lo], z_s.at[ch, m], z_r.at[ch, z],
                device(x, t, q, core), None if m else z_lo == 0,
            )

    for kind in range(2):
        for k in range(8):
            arrived(w_z.at[kind, :, k // 4, k % 4], wz_r.at[kind, k])
    for level in (6, 7):
        assemble(level, level - 6, w_z, level - 6)
    for ch in range(CHUNKS):
        for k in range(8):
            arrived(z_buf.at[ch, k // 4, k % 4], z_r.at[ch, k])
        step(6, 0, z_buf, b_buf, ch, 0)
        step(7, 1, b_buf, x_send, 0, ch)
        for i in range(4):
            t = xor(x, i, 2)
            refs = (x_send.at[ch, :, xor(t, z_lo, 2)], x_buf.at[ch, :, x])
            if i:
                send(*refs, x_s.at[ch, i], x_r.at[ch, x], device(t, y, z, core))
            else:
                keep(*refs, x_r.at[ch, x])
        if ch == 0:
            for kind in range(2):
                for k in range(8):
                    arrived(w_x.at[kind, :, k // 4, k % 4], wx_r.at[kind, k])
            for level in (8, 9, 10):
                assemble(level, level - 8, w_x, level - 8)
        for t in range(4):
            arrived(x_buf.at[ch, :, t], x_r.at[ch, t])
        step(8, 0, x_buf, b_buf, ch, 0)
        step(9, 1, b_buf, b_buf, 0, 1)
        step(10, 2, b_buf, r_send, 1, ch)
        slot = xor(z_lo, y, 2)
        lo = xor(x, z_lo, 2)
        for m in range(8):
            i, h = m % 4, m // 4
            t, hi = xor(x, i, 2), xor(z_hi, h, 1)
            send(
                r_send.at[ch, hi, t], out.at[ch, z_hi, slot], r_s.at[ch, m], r_r.at[ch, z_hi * 4 + slot],
                device(t, y, lo + 4 * hi, core), None if m else x == 0,
            )
    for ch in range(CHUNKS):
        for k in range(8):
            arrived(out.at[ch, k // 4, k % 4], r_r.at[ch, k])
    for copy, here in sent:
        if here is None:
            copy.wait_send()
        else:
            pl.when(jnp.logical_not(here))(copy.wait_send)


def interpolate(coef, leaf_out, out):
    matrix = realify(leaf_out[0], RANK)
    for ch in range(CHUNKS):
        out[0, :, pl.ds(ch * WIDTH, WIDTH)] = jnp.dot(
            matrix, coef[ch, 0], preferred_element_type=F32
        ).astype(BF16)


def body(sources, leaf_in, own_blocks, cross_blocks, leaf_out):
    sources = sources.reshape(8, 2 * LEAF, COLUMNS)
    own_blocks = own_blocks.reshape(LEVELS, 2, 4, RANK, 2 * RANK)
    cross_blocks = cross_blocks.reshape(LEVELS, 2, 4, RANK, 2 * RANK)
    dma = pltpu.SemaphoreType.DMA

    def coefs(count=CHUNKS):
        return pltpu.VMEM((count, 2, 4, 2 * RANK, WIDTH), BF16)

    def blocks(*lead):
        return pltpu.VMEM(lead + (2, 4, RANK, 2 * RANK), BF16)

    coef = pl.pallas_call(
        butterfly,
        out_shape=jax.ShapeDtypeStruct((CHUNKS, 2, 4, 2 * RANK, WIDTH), BF16),
        in_specs=[pl.BlockSpec(memory_space=pl.ANY)] * 4,
        out_specs=pl.BlockSpec(memory_space=pl.ANY),
        scratch_shapes=[
            pltpu.VMEM((8, 2 * LEAF, COLUMNS), BF16),
            pltpu.VMEM((8, RANK, 2 * LEAF), BF16),
            blocks(2, 4), blocks(), blocks(2, 2), blocks(2, 2), blocks(2, 3),
            pltpu.VMEM((LEVELS, 4, 4 * RANK, 4 * RANK), BF16),
            coefs(), coefs(2), coefs(), coefs(), coefs(), coefs(), coefs(), coefs(), coefs(), coefs(),
            dma((11,)), dma((1,)), dma((1,)), dma((2, 4)), dma((2, 4)), dma((2, 8)), dma((2, 8)), dma((2, 8)), dma((2, 8)),
            dma((CHUNKS,)), dma((CHUNKS,)), dma((CHUNKS, 4)), dma((CHUNKS, 4)), dma((CHUNKS, 8)), dma((CHUNKS, 8)),
            dma((CHUNKS, 4)), dma((CHUNKS, 4)), dma((CHUNKS, 8)), dma((CHUNKS, 8)),
        ],
        compiler_params=pltpu.CompilerParams(
            collective_id=0, has_side_effects=True, vmem_limit_bytes=44 * 2**20
        ),
        cost_estimate=pl.CostEstimate(flops=3_500_000_000, bytes_accessed=8_000_000, transcendentals=0),
        name="butterfly",
    )(sources, leaf_in, own_blocks, cross_blocks)
    coef = coef.reshape(CHUNKS, 8, 2 * RANK, WIDTH)
    result = pl.pallas_call(
        interpolate,
        out_shape=jax.ShapeDtypeStruct((8, 2 * LEAF, COLUMNS), BF16),
        grid=(8,),
        in_specs=[
            pl.BlockSpec((CHUNKS, 1, 2 * RANK, WIDTH), lambda k: (0, k, 0, 0)),
            pl.BlockSpec((1, LEAF, 2 * RANK), lambda k: (k, 0, 0)),
        ],
        out_specs=pl.BlockSpec((1, 2 * LEAF, COLUMNS), lambda k: (k, 0, 0)),
        name="interpolate",
    )(coef, leaf_out)
    return result.reshape(8, 2, LEAF, COLUMNS)


def solution(mesh):
    in_specs = (
        P(("grp", "dev"), None, None, None),
        P(("grp", "dev"), None, None),
        P(None, ("grp", "dev"), None, None),
        P(None, ("grp", "dev"), None, None),
        P(("grp", "dev"), None, None),
    )
    out_specs = P(("grp", "dev"), None, None, None)
    return jax.shard_map(body, mesh=mesh, in_specs=in_specs, out_specs=out_specs, check_vma=False)
```

```python
import functools

import jax
import jax.numpy as jnp
from jax import lax
from jax.experimental import pallas as pl
from jax.experimental.pallas import tpu as pltpu
from jax.sharding import PartitionSpec as P

RANK = 64
LEAF = 256
COLUMNS = 512
CHUNKS = 2
WIDTH = COLUMNS // CHUNKS
LEVELS = 11
MESH = pl.DeviceIdType.MESH
F32 = jnp.float32
BF16 = jnp.bfloat16


def div(a, b):
    return a // b if isinstance(a, int) else lax.div(a, jnp.int32(b))


def rem(a, b):
    return a % b if isinstance(a, int) else lax.rem(a, jnp.int32(b))


def xor(a, b, bits):
    total = 0
    for bit in range(bits):
        one, two = rem(div(a, 2**bit), 2), rem(div(b, 2**bit), 2)
        total = total + rem(one + two, 2) * 2**bit
    return total


def device(x, y, z, core):
    return {"grp": div(z, 4) * 4 + x, "dev": rem(z, 4) * 8 + y * 2 + core}


def realify(block, half):
    real_part, imag_part = block[:, :half], block[:, half:]
    upper = jnp.concatenate([real_part, -imag_part], 1)
    lower = jnp.concatenate([imag_part, real_part], 1)
    return jnp.concatenate([upper, lower], 0)


def pairs(bit):
    step = 2**bit
    return [(s, s + step) for s in range(8) if not s & step]


def butterfly(
    sources, leaf_in, own, cross, out,
    src, leaf, w_loc, w_core, w_y, w_z, w_x, big,
    a_buf, b_buf, core_buf, y_send, y_buf, v_send, v_buf, z_buf, x_send, x_buf, r_send,
    load_sem, wc_s, wc_r, wy_s, wy_r, wz_s, wz_r, wx_s, wx_r,
    c_s, c_r, y_s, y_r, v_s, v_r, z_s, z_r, x_s, x_r, r_s, r_r,
):
    grp, dev = lax.axis_index("grp"), lax.axis_index("dev")
    x, y, z = rem(grp, 4), rem(div(dev, 2), 4), div(grp, 4) * 4 + div(dev, 8)
    core = rem(dev, 2)
    z_lo, z_hi = rem(z, 4), div(z, 4)
    sent = []

    def send(from_ref, to_ref, send_sem, recv_sem, target, here=None):
        copy = pltpu.make_async_remote_copy(
            src_ref=from_ref, dst_ref=to_ref, send_sem=send_sem, recv_sem=recv_sem,
            device_id=target, device_id_type=MESH,
        )
        if here is None:
            copy.start()
        else:
            pl.when(here)(pltpu.make_async_copy(from_ref, to_ref, recv_sem).start)
            pl.when(jnp.logical_not(here))(copy.start)
        sent.append((copy, here))

    def keep(from_ref, to_ref, sem):
        pltpu.make_async_copy(from_ref, to_ref, sem).start()

    def arrived(ref, sem):
        pltpu.make_async_copy(ref, ref, sem).wait()

    kinds = (own, cross)
    loads = [pltpu.make_async_copy(leaf_in, leaf, load_sem.at[0])]
    for kind in range(2):
        loads.append(pltpu.make_async_copy(kinds[kind].at[pl.ds(0, 4)], w_loc.at[kind], load_sem.at[1 + kind]))
    for k in range(8):
        loads.append(pltpu.make_async_copy(sources.at[k], src.at[k], load_sem.at[3 + k]))
    for copy in loads:
        copy.start()

    barrier = pltpu.get_barrier_semaphore()

    def greet(target, here=None):
        def signal():
            pl.semaphore_signal(barrier, inc=1, device_id=target, device_id_type=MESH)

        if here is None:
            signal()
        else:
            pl.when(jnp.logical_not(here))(signal)

    greet(device(x, y, z, 1 - core))
    for i in range(1, 4):
        greet(device(x, xor(y, i, 2), z, core))
        greet(device(xor(x, i, 2), y, z, core))
    for m in range(1, 8):
        greet(device(x, y, xor(z, m, 3), core))
    for m in range(8):
        here = None if m else x == 0
        offset = x + 4 * (m // 4)
        greet(device(xor(x, m % 4, 2), y, xor(z, offset, 3), core), here)
        from_x = xor(x, m % 4, 2)
        greet(device(from_x, y, xor(z_lo, from_x, 2) + 4 * xor(z_hi, m // 4, 1), core), here)
    count = 1 + 6 + 7 + 16 - jnp.where(x == 0, 2, 0)

    def assemble(level, bit, w, at, p_range=range(4)):
        for p in p_range:
            s, t = pairs(bit)[p]
            def block(kind, k):
                return realify(w[kind, at, k // 4, k % 4], RANK)
            big[level, p] = jnp.concatenate(
                [
                    jnp.concatenate([block(0, s), block(1, t)], 1),
                    jnp.concatenate([block(1, s), block(0, t)], 1),
                ],
                0,
            )

    loads[1].wait()
    loads[2].wait()
    for level in range(3):
        assemble(level, level, w_loc, level)

    pl.semaphore_wait(barrier, count)

    send(cross.at[3], w_core, wc_s.at[0], wc_r.at[0], device(x, y, z, 1 - core))
    for i in range(4):
        t = xor(y, i, 2)
        for kind in range(2):
            refs = (kinds[kind].at[pl.ds(4, 2), :, t], w_y.at[kind, :, :, y])
            if i:
                send(*refs, wy_s.at[kind, i], wy_r.at[kind, y], device(x, t, z, core))
            else:
                keep(*refs, wy_r.at[kind, y])
    for m in range(8):
        q = xor(z, m, 3)
        slot, c = rem(q, 4), div(q, 4)
        for kind in range(2):
            refs = (kinds[kind].at[pl.ds(6, 2), c, slot], w_z.at[kind, :, z_hi, z_lo])
            if m:
                send(*refs, wz_s.at[kind, m], wz_r.at[kind, z], device(x, y, q, core))
            else:
                keep(*refs, wz_r.at[kind, z])
    for m in range(8):
        q = xor(z, m, 3)
        slot, c = rem(q, 4), div(q, 4)
        for kind in range(2):
            send(
                kinds[kind].at[pl.ds(8, 3), c, slot], w_x.at[kind, :, z_hi, x],
                wx_s.at[kind, m], wx_r.at[kind, x + 4 * z_hi],
                device(m % 4, y, q, core), None if m else x == 0,
            )

    loads[0].wait()
    for k in range(8):
        loads[3 + k].wait()
        value = jnp.dot(realify(leaf[k], LEAF), src[k], preferred_element_type=F32).astype(BF16)
        for ch in range(CHUNKS):
            a_buf[ch, k // 4, k % 4] = value[:, ch * WIDTH : (ch + 1) * WIDTH]

    def step(level, bit, source, target, ch_s, ch_t):
        for p, (s, t) in enumerate(pairs(bit)):
            stacked = jnp.concatenate([source[ch_s, s // 4, s % 4], source[ch_s, t // 4, t % 4]], 0)
            value = jnp.dot(big[level, p], stacked, preferred_element_type=F32).astype(BF16)
            target[ch_t, s // 4, s % 4] = value[:128]
            target[ch_t, t // 4, t % 4] = value[128:]

    for ch in range(CHUNKS):
        step(0, 0, a_buf, b_buf, ch, 0)
        step(1, 1, b_buf, b_buf, 0, 1)
        step(2, 2, b_buf, a_buf, 1, ch)
        send(a_buf.at[ch], core_buf.at[ch], c_s.at[ch], c_r.at[ch], device(x, y, z, 1 - core))

    def along_y(from_ref, to_ref, ch, send_sem, recv_sem):
        for i in (1, 2, 3, 0):
            t = xor(y, i, 2)
            refs = (from_ref.at[ch, :, t], to_ref.at[ch, :, y])
            if i:
                send(*refs, send_sem.at[ch, i], recv_sem.at[ch, y], device(x, t, z, core))
            else:
                keep(*refs, recv_sem.at[ch, y])

    def level_core(ch):
        if ch == 0:
            arrived(w_core, wc_r.at[0])
            for k in range(8):
                big[3, k // 2, pl.ds(128 * (k % 2), 128)] = jnp.concatenate(
                    [realify(w_loc[0, 3, k // 4, k % 4], RANK), realify(w_core[k // 4, k % 4], RANK)], 1
                )
        arrived(core_buf.at[ch], c_r.at[ch])
        for k in range(8):
            stacked = jnp.concatenate([a_buf[ch, k // 4, k % 4], core_buf[ch, k // 4, k % 4]], 0)
            y_send[ch, k // 4, k % 4] = jnp.dot(
                big[3, k // 2, pl.ds(128 * (k % 2), 128)], stacked, preferred_element_type=F32
            ).astype(BF16)
        along_y(y_send, y_buf, ch, y_s, y_r)

    def levels_y(ch):
        if ch == 0:
            for kind in range(2):
                for t in range(4):
                    arrived(w_y.at[kind, :, :, t], wy_r.at[kind, t])
            for level in (4, 5):
                assemble(level, level - 4, w_y, level - 4)
        for t in range(4):
            arrived(y_buf.at[ch, :, t], y_r.at[ch, t])
        step(4, 0, y_buf, b_buf, ch, 0)
        step(5, 1, b_buf, v_send, 0, ch)
        along_y(v_send, v_buf, ch, v_s, v_r)

    def to_z(ch):
        for t in range(4):
            arrived(v_buf.at[ch, :, t], v_r.at[ch, t])
        for m in (4, 3, 5, 2, 6, 1, 7, 0):
            q = xor(z, m, 3)
            refs = (v_buf.at[ch, div(q, 4), rem(q, 4)], z_buf.at[ch, z_hi, z_lo])
            if m:
                send(*refs, z_s.at[ch, m], z_r.at[ch, z], device(x, y, q, core))
            else:
                keep(*refs, z_r.at[ch, z])

    def levels_z(ch):
        if ch == 0:
            for kind in range(2):
                for k in range(8):
                    arrived(w_z.at[kind, :, k // 4, k % 4], wz_r.at[kind, k])
            for level in (6, 7):
                assemble(level, level - 6, w_z, level - 6)
        for k in range(8):
            arrived(z_buf.at[ch, k // 4, k % 4], z_r.at[ch, k])
        step(6, 0, z_buf, b_buf, ch, 0)
        step(7, 1, b_buf, x_send, 0, ch)
        for i in (1, 2, 3, 0):
            t = xor(x, i, 2)
            refs = (x_send.at[ch, :, xor(t, z_lo, 2)], x_buf.at[ch, :, x])
            if i:
                send(*refs, x_s.at[ch, i], x_r.at[ch, x], device(t, y, z, core))
            else:
                keep(*refs, x_r.at[ch, x])

    def levels_x(ch):
        if ch == 0:
            for kind in range(2):
                for k in range(8):
                    arrived(w_x.at[kind, :, k // 4, k % 4], wx_r.at[kind, k])
            for level in (8, 9, 10):
                assemble(level, level - 8, w_x, level - 8)
        for t in range(4):
            arrived(x_buf.at[ch, :, t], x_r.at[ch, t])
        step(8, 0, x_buf, b_buf, ch, 0)
        step(9, 1, b_buf, b_buf, 0, 1)
        step(10, 2, b_buf, r_send, 1, ch)
        lo = xor(x, z_lo, 2)
        for m in (4, 3, 5, 2, 6, 1, 7, 0):
            t, hi = xor(x, m % 4, 2), xor(z_hi, m // 4, 1)
            send(
                r_send.at[ch, hi, t], out.at[ch, z_hi, z_lo], r_s.at[ch, m], r_r.at[ch, z],
                device(t, y, lo + 4 * hi, core), None if m else x == 0,
            )

    for ch in range(CHUNKS):
        level_core(ch)
    levels_y(0)
    for ch in range(1, CHUNKS):
        levels_y(ch)
        to_z(ch - 1)
    to_z(CHUNKS - 1)
    for ch in range(CHUNKS):
        levels_z(ch)
        levels_x(ch)
    for ch in range(CHUNKS):
        for k in range(8):
            arrived(out.at[ch, k // 4, k % 4], r_r.at[ch, k])
    for copy, here in sent:
        if here is None:
            copy.wait_send()
        else:
            pl.when(jnp.logical_not(here))(copy.wait_send)


def interpolate(coef, leaf_out, out, coef_buf, leaf_buf, out_buf, in_sem, out_sem):
    loads = [
        (
            pltpu.make_async_copy(coef.at[:, k], coef_buf.at[:, k], in_sem.at[0, k]),
            pltpu.make_async_copy(leaf_out.at[k], leaf_buf.at[k], in_sem.at[1, k]),
        )
        for k in range(8)
    ]
    for pair in loads:
        for copy in pair:
            copy.start()
    stores = []
    for k in range(8):
        for copy in loads[k]:
            copy.wait()
        values = jnp.concatenate([coef_buf[ch, k] for ch in range(CHUNKS)], 1)
        out_buf[k] = jnp.dot(
            realify(leaf_buf[k], RANK), values, preferred_element_type=F32
        ).astype(BF16)
        stores.append(pltpu.make_async_copy(out_buf.at[k], out.at[k], out_sem.at[k]))
        stores[k].start()
    for copy in stores:
        copy.wait()


def body(sources, leaf_in, own_blocks, cross_blocks, leaf_out):
    sources = sources.reshape(8, 2 * LEAF, COLUMNS)
    own_blocks = own_blocks.reshape(LEVELS, 2, 4, RANK, 2 * RANK)
    cross_blocks = cross_blocks.reshape(LEVELS, 2, 4, RANK, 2 * RANK)
    dma = pltpu.SemaphoreType.DMA

    def coefs(count=CHUNKS):
        return pltpu.VMEM((count, 2, 4, 2 * RANK, WIDTH), BF16)

    def blocks(*lead):
        return pltpu.VMEM(lead + (2, 4, RANK, 2 * RANK), BF16)

    coef = pl.pallas_call(
        butterfly,
        out_shape=jax.ShapeDtypeStruct((CHUNKS, 2, 4, 2 * RANK, WIDTH), BF16),
        in_specs=[pl.BlockSpec(memory_space=pltpu.HBM)] * 4,
        out_specs=pl.BlockSpec(memory_space=pl.ANY),
        scratch_shapes=[
            pltpu.VMEM((8, 2 * LEAF, COLUMNS), BF16),
            pltpu.VMEM((8, RANK, 2 * LEAF), BF16),
            blocks(2, 4), blocks(), blocks(2, 2), blocks(2, 2), blocks(2, 3),
            pltpu.VMEM((LEVELS, 4, 4 * RANK, 4 * RANK), BF16),
            coefs(), coefs(2), coefs(), coefs(), coefs(), coefs(), coefs(), coefs(), coefs(), coefs(), coefs(),
            dma((11,)), dma((1,)), dma((1,)), dma((2, 4)), dma((2, 4)), dma((2, 8)), dma((2, 8)), dma((2, 8)), dma((2, 8)),
            dma((CHUNKS,)), dma((CHUNKS,)), dma((CHUNKS, 4)), dma((CHUNKS, 4)), dma((CHUNKS, 4)), dma((CHUNKS, 4)), dma((CHUNKS, 8)), dma((CHUNKS, 8)),
            dma((CHUNKS, 4)), dma((CHUNKS, 4)), dma((CHUNKS, 8)), dma((CHUNKS, 8)),
        ],
        compiler_params=pltpu.CompilerParams(
            collective_id=0, has_side_effects=True, vmem_limit_bytes=60 * 2**20
        ),
        cost_estimate=pl.CostEstimate(flops=3_500_000_000, bytes_accessed=8_000_000, transcendentals=0),
        name="butterfly",
    )(sources, leaf_in, own_blocks, cross_blocks)
    coef = coef.reshape(CHUNKS, 8, 2 * RANK, WIDTH)
    result = pl.pallas_call(
        interpolate,
        out_shape=jax.ShapeDtypeStruct((8, 2 * LEAF, COLUMNS), BF16),
        in_specs=[pl.BlockSpec(memory_space=pltpu.HBM)] * 2,
        out_specs=pl.BlockSpec(memory_space=pltpu.HBM),
        scratch_shapes=[
            pltpu.VMEM((CHUNKS, 8, 2 * RANK, WIDTH), BF16),
            pltpu.VMEM((8, LEAF, 2 * RANK), BF16),
            pltpu.VMEM((8, 2 * LEAF, COLUMNS), BF16),
            dma((2, 8)), dma((8,)),
        ],
        compiler_params=pltpu.CompilerParams(vmem_limit_bytes=60 * 2**20),
        name="interpolate",
    )(coef, leaf_out)
    return result.reshape(8, 2, LEAF, COLUMNS)


def solution(mesh):
    in_specs = (
        P(("grp", "dev"), None, None, None),
        P(("grp", "dev"), None, None),
        P(None, ("grp", "dev"), None, None),
        P(None, ("grp", "dev"), None, None),
        P(("grp", "dev"), None, None),
    )
    out_specs = P(("grp", "dev"), None, None, None)
    return jax.shard_map(body, mesh=mesh, in_specs=in_specs, out_specs=out_specs, check_vma=False)
```

```python
import functools

import jax
import jax.numpy as jnp
from jax import lax
from jax.experimental import pallas as pl
from jax.experimental.pallas import tpu as pltpu
from jax.sharding import PartitionSpec as P

RANK = 64
LEAF = 256
COLUMNS = 512
CHUNKS = 2
WIDTH = COLUMNS // CHUNKS
LEVELS = 11
MESH = pl.DeviceIdType.MESH
F32 = jnp.float32
BF16 = jnp.bfloat16


def div(a, b):
    return a // b if isinstance(a, int) else lax.div(a, jnp.int32(b))


def rem(a, b):
    return a % b if isinstance(a, int) else lax.rem(a, jnp.int32(b))


def xor(a, b, bits):
    total = 0
    for bit in range(bits):
        one, two = rem(div(a, 2**bit), 2), rem(div(b, 2**bit), 2)
        total = total + rem(one + two, 2) * 2**bit
    return total


def device(x, y, z, core):
    return {"grp": div(z, 4) * 4 + x, "dev": rem(z, 4) * 8 + y * 2 + core}


def realify(block, half):
    real_part, imag_part = block[:, :half], block[:, half:]
    upper = jnp.concatenate([real_part, -imag_part], 1)
    lower = jnp.concatenate([imag_part, real_part], 1)
    return jnp.concatenate([upper, lower], 0)


def pairs(bit):
    step = 2**bit
    return [(s, s + step) for s in range(8) if not s & step]


def butterfly(
    sources, leaf_in, own, cross, out,
    src, leaf, w_loc, w_core, w_y, w_z, w_x, big,
    a_buf, b_buf, core_buf, y_send, y_buf, v_send, v_buf, z_buf, x_send, x_buf, r_send,
    load_sem, wc_s, wc_r, wy_s, wy_r, wz_s, wz_r, wx_s, wx_r,
    c_s, c_r, y_s, y_r, v_s, v_r, z_s, z_r, x_s, x_r, r_s, r_r,
):
    grp, dev = lax.axis_index("grp"), lax.axis_index("dev")
    x, y, z = rem(grp, 4), rem(div(dev, 2), 4), div(grp, 4) * 4 + div(dev, 8)
    core = rem(dev, 2)
    z_lo, z_hi = rem(z, 4), div(z, 4)
    sent = []

    def send(from_ref, to_ref, send_sem, recv_sem, target, here=None):
        copy = pltpu.make_async_remote_copy(
            src_ref=from_ref, dst_ref=to_ref, send_sem=send_sem, recv_sem=recv_sem,
            device_id=target, device_id_type=MESH,
        )
        if here is None:
            copy.start()
        else:
            pl.when(here)(pltpu.make_async_copy(from_ref, to_ref, recv_sem).start)
            pl.when(jnp.logical_not(here))(copy.start)
        sent.append((copy, here))

    def keep(from_ref, to_ref, sem):
        pltpu.make_async_copy(from_ref, to_ref, sem).start()

    def arrived(ref, sem):
        pltpu.make_async_copy(ref, ref, sem).wait()

    kinds = (own, cross)
    loads = [pltpu.make_async_copy(leaf_in, leaf, load_sem.at[0])]
    for kind in range(2):
        loads.append(pltpu.make_async_copy(kinds[kind].at[pl.ds(0, 4)], w_loc.at[kind], load_sem.at[1 + kind]))
    for k in range(8):
        loads.append(pltpu.make_async_copy(sources.at[k], src.at[k], load_sem.at[3 + k]))
    for copy in loads:
        copy.start()

    barrier = pltpu.get_barrier_semaphore()

    def greet(target, here=None):
        def signal():
            pl.semaphore_signal(barrier, inc=1, device_id=target, device_id_type=MESH)

        if here is None:
            signal()
        else:
            pl.when(jnp.logical_not(here))(signal)

    greet(device(x, y, z, 1 - core))
    for i in range(1, 4):
        greet(device(x, xor(y, i, 2), z, core))
        greet(device(xor(x, i, 2), y, z, core))
    for m in range(1, 8):
        greet(device(x, y, xor(z, m, 3), core))
    for m in range(8):
        here = None if m else x == 0
        offset = x + 4 * (m // 4)
        greet(device(xor(x, m % 4, 2), y, xor(z, offset, 3), core), here)
        from_x = xor(x, m % 4, 2)
        greet(device(from_x, y, xor(z_lo, from_x, 2) + 4 * xor(z_hi, m // 4, 1), core), here)
    count = 1 + 6 + 7 + 16 - jnp.where(x == 0, 2, 0)

    pl.semaphore_wait(barrier, count)

    for m in range(8):
        q = xor(z, m, 3)
        slot, c = rem(q, 4), div(q, 4)
        for kind in range(2):
            refs = (kinds[kind].at[pl.ds(6, 2), c, slot], w_z.at[kind, :, z_hi, z_lo])
            if m:
                send(*refs, wz_s.at[kind, m], wz_r.at[kind, z], device(x, y, q, core))
            else:
                keep(*refs, wz_r.at[kind, z])
    for m in range(8):
        q = xor(z, m, 3)
        slot, c = rem(q, 4), div(q, 4)
        for kind in range(2):
            send(
                kinds[kind].at[pl.ds(8, 3), c, slot], w_x.at[kind, :, z_hi, x],
                wx_s.at[kind, m], wx_r.at[kind, x + 4 * z_hi],
                device(m % 4, y, q, core), None if m else x == 0,
            )
    send(cross.at[3], w_core, wc_s.at[0], wc_r.at[0], device(x, y, z, 1 - core))
    for i in range(4):
        t = xor(y, i, 2)
        for kind in range(2):
            refs = (kinds[kind].at[pl.ds(4, 2), :, t], w_y.at[kind, :, :, y])
            if i:
                send(*refs, wy_s.at[kind, i], wy_r.at[kind, y], device(x, t, z, core))
            else:
                keep(*refs, wy_r.at[kind, y])

    def assemble(level, bit, w, at, p_range=range(4)):
        for p in p_range:
            s, t = pairs(bit)[p]
            def block(kind, k):
                return realify(w[kind, at, k // 4, k % 4], RANK)
            big[level, p] = jnp.concatenate(
                [
                    jnp.concatenate([block(0, s), block(1, t)], 1),
                    jnp.concatenate([block(1, s), block(0, t)], 1),
                ],
                0,
            )

    loads[1].wait()
    loads[2].wait()
    for level in range(3):
        assemble(level, level, w_loc, level)

    loads[0].wait()
    for k in range(8):
        loads[3 + k].wait()
        value = jnp.dot(realify(leaf[k], LEAF), src[k], preferred_element_type=F32).astype(BF16)
        for ch in range(CHUNKS):
            a_buf[ch, k // 4, k % 4] = value[:, ch * WIDTH : (ch + 1) * WIDTH]

    def step(level, bit, source, target, ch_s, ch_t):
        for p, (s, t) in enumerate(pairs(bit)):
            stacked = jnp.concatenate([source[ch_s, s // 4, s % 4], source[ch_s, t // 4, t % 4]], 0)
            value = jnp.dot(big[level, p], stacked, preferred_element_type=F32).astype(BF16)
            target[ch_t, s // 4, s % 4] = value[:128]
            target[ch_t, t // 4, t % 4] = value[128:]

    for ch in range(CHUNKS):
        step(0, 0, a_buf, b_buf, ch, 0)
        step(1, 1, b_buf, b_buf, 0, 1)
        step(2, 2, b_buf, a_buf, 1, ch)
        send(a_buf.at[ch], core_buf.at[ch], c_s.at[ch], c_r.at[ch], device(x, y, z, 1 - core))

    def along_y(from_ref, to_ref, ch, send_sem, recv_sem):
        for i in (1, 2, 3, 0):
            t = xor(y, i, 2)
            refs = (from_ref.at[ch, :, t], to_ref.at[ch, :, y])
            if i:
                send(*refs, send_sem.at[ch, i], recv_sem.at[ch, y], device(x, t, z, core))
            else:
                keep(*refs, recv_sem.at[ch, y])

    def level_core(ch):
        if ch == 0:
            arrived(w_core, wc_r.at[0])
            for k in range(8):
                big[3, k // 2, pl.ds(128 * (k % 2), 128)] = jnp.concatenate(
                    [realify(w_loc[0, 3, k // 4, k % 4], RANK), realify(w_core[k // 4, k % 4], RANK)], 1
                )
        arrived(core_buf.at[ch], c_r.at[ch])
        for k in range(8):
            stacked = jnp.concatenate([a_buf[ch, k // 4, k % 4], core_buf[ch, k // 4, k % 4]], 0)
            y_send[ch, k // 4, k % 4] = jnp.dot(
                big[3, k // 2, pl.ds(128 * (k % 2), 128)], stacked, preferred_element_type=F32
            ).astype(BF16)
        along_y(y_send, y_buf, ch, y_s, y_r)

    def levels_y(ch):
        if ch == 0:
            for kind in range(2):
                for t in range(4):
                    arrived(w_y.at[kind, :, :, t], wy_r.at[kind, t])
            for level in (4, 5):
                assemble(level, level - 4, w_y, level - 4)
        for t in range(4):
            arrived(y_buf.at[ch, :, t], y_r.at[ch, t])
        step(4, 0, y_buf, b_buf, ch, 0)
        step(5, 1, b_buf, v_send, 0, ch)
        along_y(v_send, v_buf, ch, v_s, v_r)

    def to_z(ch):
        for t in range(4):
            arrived(v_buf.at[ch, :, t], v_r.at[ch, t])
        for m in (4, 3, 5, 2, 6, 1, 7, 0):
            q = xor(z, m, 3)
            refs = (v_buf.at[ch, div(q, 4), rem(q, 4)], z_buf.at[ch, z_hi, z_lo])
            if m:
                send(*refs, z_s.at[ch, m], z_r.at[ch, z], device(x, y, q, core))
            else:
                keep(*refs, z_r.at[ch, z])

    def levels_z(ch):
        if ch == 0:
            for kind in range(2):
                for k in range(8):
                    arrived(w_z.at[kind, :, k // 4, k % 4], wz_r.at[kind, k])
            for level in (6, 7):
                assemble(level, level - 6, w_z, level - 6)
        for k in range(8):
            arrived(z_buf.at[ch, k // 4, k % 4], z_r.at[ch, k])
        step(6, 0, z_buf, b_buf, ch, 0)
        step(7, 1, b_buf, x_send, 0, ch)
        for i in (1, 2, 3, 0):
            t = xor(x, i, 2)
            refs = (x_send.at[ch, :, xor(t, z_lo, 2)], x_buf.at[ch, :, x])
            if i:
                send(*refs, x_s.at[ch, i], x_r.at[ch, x], device(t, y, z, core))
            else:
                keep(*refs, x_r.at[ch, x])

    def levels_x(ch):
        if ch == 0:
            for kind in range(2):
                for k in range(8):
                    arrived(w_x.at[kind, :, k // 4, k % 4], wx_r.at[kind, k])
            for level in (8, 9, 10):
                assemble(level, level - 8, w_x, level - 8)
        for t in range(4):
            arrived(x_buf.at[ch, :, t], x_r.at[ch, t])
        step(8, 0, x_buf, b_buf, ch, 0)
        step(9, 1, b_buf, b_buf, 0, 1)
        step(10, 2, b_buf, r_send, 1, ch)
        lo = xor(x, z_lo, 2)
        for m in (4, 3, 5, 2, 6, 1, 7, 0):
            t, hi = xor(x, m % 4, 2), xor(z_hi, m // 4, 1)
            send(
                r_send.at[ch, hi, t], out.at[ch, z_hi, z_lo], r_s.at[ch, m], r_r.at[ch, z],
                device(t, y, lo + 4 * hi, core), None if m else x == 0,
            )

    level_core(0)
    levels_y(0)
    level_core(1)
    to_z(0)
    levels_y(1)
    to_z(1)
    for ch in range(CHUNKS):
        levels_z(ch)
        levels_x(ch)
    for ch in range(CHUNKS):
        for k in range(8):
            arrived(out.at[ch, k // 4, k % 4], r_r.at[ch, k])
    for copy, here in sent:
        if here is None:
            copy.wait_send()
        else:
            pl.when(jnp.logical_not(here))(copy.wait_send)


def interpolate(coef, leaf_out, out, coef_buf, leaf_buf, out_buf, in_sem, out_sem):
    loads = [
        (
            pltpu.make_async_copy(coef.at[:, k], coef_buf.at[:, k], in_sem.at[0, k]),
            pltpu.make_async_copy(leaf_out.at[k], leaf_buf.at[k], in_sem.at[1, k]),
        )
        for k in range(8)
    ]
    for pair in loads:
        for copy in pair:
            copy.start()
    stores = []
    for k in range(8):
        for copy in loads[k]:
            copy.wait()
        values = jnp.concatenate([coef_buf[ch, k] for ch in range(CHUNKS)], 1)
        out_buf[k] = jnp.dot(
            realify(leaf_buf[k], RANK), values, preferred_element_type=F32
        ).astype(BF16)
        stores.append(pltpu.make_async_copy(out_buf.at[k], out.at[k], out_sem.at[k]))
        stores[k].start()
    for copy in stores:
        copy.wait()


def body(sources, leaf_in, own_blocks, cross_blocks, leaf_out):
    sources = sources.reshape(8, 2 * LEAF, COLUMNS)
    own_blocks = own_blocks.reshape(LEVELS, 2, 4, RANK, 2 * RANK)
    cross_blocks = cross_blocks.reshape(LEVELS, 2, 4, RANK, 2 * RANK)
    dma = pltpu.SemaphoreType.DMA

    def coefs(count=CHUNKS):
        return pltpu.VMEM((count, 2, 4, 2 * RANK, WIDTH), BF16)

    def blocks(*lead):
        return pltpu.VMEM(lead + (2, 4, RANK, 2 * RANK), BF16)

    coef = pl.pallas_call(
        butterfly,
        out_shape=jax.ShapeDtypeStruct((CHUNKS, 2, 4, 2 * RANK, WIDTH), BF16),
        in_specs=[pl.BlockSpec(memory_space=pltpu.HBM)] * 4,
        out_specs=pl.BlockSpec(memory_space=pl.ANY),
        scratch_shapes=[
            pltpu.VMEM((8, 2 * LEAF, COLUMNS), BF16),
            pltpu.VMEM((8, RANK, 2 * LEAF), BF16),
            blocks(2, 4), blocks(), blocks(2, 2), blocks(2, 2), blocks(2, 3),
            pltpu.VMEM((LEVELS, 4, 4 * RANK, 4 * RANK), BF16),
            coefs(), coefs(2), coefs(), coefs(), coefs(), coefs(), coefs(), coefs(), coefs(), coefs(), coefs(),
            dma((11,)), dma((1,)), dma((1,)), dma((2, 4)), dma((2, 4)), dma((2, 8)), dma((2, 8)), dma((2, 8)), dma((2, 8)),
            dma((CHUNKS,)), dma((CHUNKS,)), dma((CHUNKS, 4)), dma((CHUNKS, 4)), dma((CHUNKS, 4)), dma((CHUNKS, 4)), dma((CHUNKS, 8)), dma((CHUNKS, 8)),
            dma((CHUNKS, 4)), dma((CHUNKS, 4)), dma((CHUNKS, 8)), dma((CHUNKS, 8)),
        ],
        compiler_params=pltpu.CompilerParams(
            collective_id=0, has_side_effects=True, vmem_limit_bytes=60 * 2**20
        ),
        cost_estimate=pl.CostEstimate(flops=3_500_000_000, bytes_accessed=8_000_000, transcendentals=0),
        name="butterfly",
    )(sources, leaf_in, own_blocks, cross_blocks)
    coef = coef.reshape(CHUNKS, 8, 2 * RANK, WIDTH)
    result = pl.pallas_call(
        interpolate,
        out_shape=jax.ShapeDtypeStruct((8, 2 * LEAF, COLUMNS), BF16),
        in_specs=[pl.BlockSpec(memory_space=pltpu.HBM)] * 2,
        out_specs=pl.BlockSpec(memory_space=pltpu.HBM),
        scratch_shapes=[
            pltpu.VMEM((CHUNKS, 8, 2 * RANK, WIDTH), BF16),
            pltpu.VMEM((8, LEAF, 2 * RANK), BF16),
            pltpu.VMEM((8, 2 * LEAF, COLUMNS), BF16),
            dma((2, 8)), dma((8,)),
        ],
        compiler_params=pltpu.CompilerParams(vmem_limit_bytes=60 * 2**20),
        name="interpolate",
    )(coef, leaf_out)
    return result.reshape(8, 2, LEAF, COLUMNS)


def solution(mesh):
    in_specs = (
        P(("grp", "dev"), None, None, None),
        P(("grp", "dev"), None, None),
        P(None, ("grp", "dev"), None, None),
        P(None, ("grp", "dev"), None, None),
        P(("grp", "dev"), None, None),
    )
    out_specs = P(("grp", "dev"), None, None, None)
    return jax.shard_map(body, mesh=mesh, in_specs=in_specs, out_specs=out_specs, check_vma=False)
```

```python
import functools

import jax
import jax.numpy as jnp
from jax import lax
from jax.experimental import pallas as pl
from jax.experimental.pallas import tpu as pltpu
from jax.sharding import PartitionSpec as P

RANK = 64
LEAF = 256
COLUMNS = 512
CHUNKS = 2
WIDTH = COLUMNS // CHUNKS
LEVELS = 11
MESH = pl.DeviceIdType.MESH
F32 = jnp.float32
BF16 = jnp.bfloat16


def div(a, b):
    return a // b if isinstance(a, int) else lax.div(a, jnp.int32(b))


def rem(a, b):
    return a % b if isinstance(a, int) else lax.rem(a, jnp.int32(b))


def xor(a, b, bits):
    total = 0
    for bit in range(bits):
        one, two = rem(div(a, 2**bit), 2), rem(div(b, 2**bit), 2)
        total = total + rem(one + two, 2) * 2**bit
    return total


def device(x, y, z, core):
    return {"grp": div(z, 4) * 4 + x, "dev": rem(z, 4) * 8 + y * 2 + core}


def realify(block, half):
    real_part, imag_part = block[:, :half], block[:, half:]
    upper = jnp.concatenate([real_part, -imag_part], 1)
    lower = jnp.concatenate([imag_part, real_part], 1)
    return jnp.concatenate([upper, lower], 0)


def pairs(bit):
    step = 2**bit
    return [(s, s + step) for s in range(8) if not s & step]


def butterfly(
    sources, leaf_in, own, cross, out,
    src, leaf, w_loc, w_core, w_y, w_z, w_x, big,
    a_buf, b_buf, core_buf, y_send, y_buf, v_send, v_buf, z_buf, x_send, x_buf, r_send,
    load_sem, wc_s, wc_r, wy_s, wy_r, wz_s, wz_r, wx_s, wx_r,
    c_s, c_r, y_s, y_r, v_s, v_r, z_s, z_r, x_s, x_r, r_s, r_r,
):
    grp, dev = lax.axis_index("grp"), lax.axis_index("dev")
    x, y, z = rem(grp, 4), rem(div(dev, 2), 4), div(grp, 4) * 4 + div(dev, 8)
    core = rem(dev, 2)
    z_lo, z_hi = rem(z, 4), div(z, 4)
    sent = []

    def send(from_ref, to_ref, send_sem, recv_sem, target, here=None):
        copy = pltpu.make_async_remote_copy(
            src_ref=from_ref, dst_ref=to_ref, send_sem=send_sem, recv_sem=recv_sem,
            device_id=target, device_id_type=MESH,
        )
        if here is None:
            copy.start()
        else:
            pl.when(here)(pltpu.make_async_copy(from_ref, to_ref, recv_sem).start)
            pl.when(jnp.logical_not(here))(copy.start)
        sent.append((copy, here))

    def keep(from_ref, to_ref, sem):
        pltpu.make_async_copy(from_ref, to_ref, sem).start()

    def arrived(ref, sem):
        pltpu.make_async_copy(ref, ref, sem).wait()

    kinds = (own, cross)
    loads = [pltpu.make_async_copy(leaf_in, leaf, load_sem.at[0])]
    for kind in range(2):
        loads.append(pltpu.make_async_copy(kinds[kind].at[pl.ds(0, 4)], w_loc.at[kind], load_sem.at[1 + kind]))
    for k in range(8):
        loads.append(pltpu.make_async_copy(sources.at[k], src.at[k], load_sem.at[3 + k]))
    for copy in loads:
        copy.start()

    barrier = pltpu.get_barrier_semaphore()

    def greet(target, here=None):
        def signal():
            pl.semaphore_signal(barrier, inc=1, device_id=target, device_id_type=MESH)

        if here is None:
            signal()
        else:
            pl.when(jnp.logical_not(here))(signal)

    greet(device(x, y, z, 1 - core))
    for i in range(1, 4):
        greet(device(x, xor(y, i, 2), z, core))
        greet(device(xor(x, i, 2), y, z, core))
    for m in range(1, 8):
        greet(device(x, y, xor(z, m, 3), core))
    for m in range(8):
        here = None if m else x == 0
        offset = x + 4 * (m // 4)
        greet(device(xor(x, m % 4, 2), y, xor(z, offset, 3), core), here)
        from_x = xor(x, m % 4, 2)
        greet(device(from_x, y, xor(z_lo, from_x, 2) + 4 * xor(z_hi, m // 4, 1), core), here)
    count = 1 + 6 + 7 + 16 - jnp.where(x == 0, 2, 0)

    pl.semaphore_wait(barrier, count)

    for m in range(8):
        q = xor(z, m, 3)
        slot, c = rem(q, 4), div(q, 4)
        for kind in range(2):
            refs = (kinds[kind].at[pl.ds(6, 2), c, slot], w_z.at[kind, :, z_hi, z_lo])
            if m:
                send(*refs, wz_s.at[kind, m], wz_r.at[kind, z], device(x, y, q, core))
            else:
                keep(*refs, wz_r.at[kind, z])
    for m in range(8):
        q = xor(z, m, 3)
        slot, c = rem(q, 4), div(q, 4)
        for kind in range(2):
            send(
                kinds[kind].at[pl.ds(8, 3), c, slot], w_x.at[kind, :, z_hi, x],
                wx_s.at[kind, m], wx_r.at[kind, x + 4 * z_hi],
                device(m % 4, y, q, core), None if m else x == 0,
            )
    send(cross.at[3], w_core, wc_s.at[0], wc_r.at[0], device(x, y, z, 1 - core))
    for i in range(4):
        t = xor(y, i, 2)
        for kind in range(2):
            refs = (kinds[kind].at[pl.ds(4, 2), :, t], w_y.at[kind, :, :, y])
            if i:
                send(*refs, wy_s.at[kind, i], wy_r.at[kind, y], device(x, t, z, core))
            else:
                keep(*refs, wy_r.at[kind, y])

    def assemble(level, bit, w, at, p_range=range(4)):
        for p in p_range:
            s, t = pairs(bit)[p]
            def block(kind, k):
                return realify(w[kind, at, k // 4, k % 4], RANK)
            big[level, p] = jnp.concatenate(
                [
                    jnp.concatenate([block(0, s), block(1, t)], 1),
                    jnp.concatenate([block(1, s), block(0, t)], 1),
                ],
                0,
            )

    loads[1].wait()
    loads[2].wait()
    for level in range(3):
        assemble(level, level, w_loc, level)

    def step(level, bit, source, target, ch_s, ch_t):
        for p, (s, t) in enumerate(pairs(bit)):
            stacked = jnp.concatenate([source[ch_s, s // 4, s % 4], source[ch_s, t // 4, t % 4]], 0)
            value = jnp.dot(big[level, p], stacked, preferred_element_type=F32).astype(BF16)
            target[ch_t, s // 4, s % 4] = value[:128]
            target[ch_t, t // 4, t % 4] = value[128:]

    def levels_local(ch):
        if ch == 0:
            loads[0].wait()
        for k in range(8):
            if ch == 0:
                loads[3 + k].wait()
            a_buf[ch, k // 4, k % 4] = jnp.dot(
                realify(leaf[k], LEAF), src[k, :, ch * WIDTH : (ch + 1) * WIDTH], preferred_element_type=F32
            ).astype(BF16)
        step(0, 0, a_buf, b_buf, ch, 0)
        step(1, 1, b_buf, b_buf, 0, 1)
        step(2, 2, b_buf, a_buf, 1, ch)
        send(a_buf.at[ch], core_buf.at[ch], c_s.at[ch], c_r.at[ch], device(x, y, z, 1 - core))

    def along_y(from_ref, to_ref, ch, send_sem, recv_sem):
        for i in (1, 2, 3, 0):
            t = xor(y, i, 2)
            refs = (from_ref.at[ch, :, t], to_ref.at[ch, :, y])
            if i:
                send(*refs, send_sem.at[ch, i], recv_sem.at[ch, y], device(x, t, z, core))
            else:
                keep(*refs, recv_sem.at[ch, y])

    def level_core(ch):
        if ch == 0:
            arrived(w_core, wc_r.at[0])
            for k in range(8):
                big[3, k // 2, pl.ds(128 * (k % 2), 128)] = jnp.concatenate(
                    [realify(w_loc[0, 3, k // 4, k % 4], RANK), realify(w_core[k // 4, k % 4], RANK)], 1
                )
        arrived(core_buf.at[ch], c_r.at[ch])
        for k in range(8):
            stacked = jnp.concatenate([a_buf[ch, k // 4, k % 4], core_buf[ch, k // 4, k % 4]], 0)
            y_send[ch, k // 4, k % 4] = jnp.dot(
                big[3, k // 2, pl.ds(128 * (k % 2), 128)], stacked, preferred_element_type=F32
            ).astype(BF16)
        along_y(y_send, y_buf, ch, y_s, y_r)

    def levels_y(ch):
        if ch == 0:
            for kind in range(2):
                for t in range(4):
                    arrived(w_y.at[kind, :, :, t], wy_r.at[kind, t])
            for level in (4, 5):
                assemble(level, level - 4, w_y, level - 4)
        for t in range(4):
            arrived(y_buf.at[ch, :, t], y_r.at[ch, t])
        step(4, 0, y_buf, b_buf, ch, 0)
        step(5, 1, b_buf, v_send, 0, ch)
        along_y(v_send, v_buf, ch, v_s, v_r)

    def to_z(ch):
        for t in range(4):
            arrived(v_buf.at[ch, :, t], v_r.at[ch, t])
        for m in (4, 3, 5, 2, 6, 1, 7, 0):
            q = xor(z, m, 3)
            refs = (v_buf.at[ch, div(q, 4), rem(q, 4)], z_buf.at[ch, z_hi, z_lo])
            if m:
                send(*refs, z_s.at[ch, m], z_r.at[ch, z], device(x, y, q, core))
            else:
                keep(*refs, z_r.at[ch, z])

    def levels_z(ch):
        if ch == 0:
            for kind in range(2):
                for k in range(8):
                    arrived(w_z.at[kind, :, k // 4, k % 4], wz_r.at[kind, k])
            for level in (6, 7):
                assemble(level, level - 6, w_z, level - 6)
        for k in range(8):
            arrived(z_buf.at[ch, k // 4, k % 4], z_r.at[ch, k])
        step(6, 0, z_buf, b_buf, ch, 0)
        step(7, 1, b_buf, x_send, 0, ch)
        for i in (1, 2, 3, 0):
            t = xor(x, i, 2)
            refs = (x_send.at[ch, :, xor(t, z_lo, 2)], x_buf.at[ch, :, x])
            if i:
                send(*refs, x_s.at[ch, i], x_r.at[ch, x], device(t, y, z, core))
            else:
                keep(*refs, x_r.at[ch, x])

    def levels_x(ch):
        if ch == 0:
            for kind in range(2):
                for k in range(8):
                    arrived(w_x.at[kind, :, k // 4, k % 4], wx_r.at[kind, k])
            for level in (8, 9, 10):
                assemble(level, level - 8, w_x, level - 8)
        for t in range(4):
            arrived(x_buf.at[ch, :, t], x_r.at[ch, t])
        step(8, 0, x_buf, b_buf, ch, 0)
        step(9, 1, b_buf, b_buf, 0, 1)
        step(10, 2, b_buf, r_send, 1, ch)
        lo = xor(x, z_lo, 2)
        for m in (4, 3, 5, 2, 6, 1, 7, 0):
            t, hi = xor(x, m % 4, 2), xor(z_hi, m // 4, 1)
            send(
                r_send.at[ch, hi, t], out.at[ch, z_hi, z_lo], r_s.at[ch, m], r_r.at[ch, z],
                device(t, y, lo + 4 * hi, core), None if m else x == 0,
            )

    levels_local(0)
    levels_local(1)
    level_core(0)
    levels_y(0)
    level_core(1)
    to_z(0)
    levels_y(1)
    to_z(1)
    for ch in range(CHUNKS):
        levels_z(ch)
        levels_x(ch)
    for ch in range(CHUNKS):
        for k in range(8):
            arrived(out.at[ch, k // 4, k % 4], r_r.at[ch, k])
    for copy, here in sent:
        if here is None:
            copy.wait_send()
        else:
            pl.when(jnp.logical_not(here))(copy.wait_send)


def interpolate(coef, leaf_out, out, coef_buf, leaf_buf, out_buf, in_sem, out_sem):
    loads = [
        (
            pltpu.make_async_copy(coef.at[:, k], coef_buf.at[:, k], in_sem.at[0, k]),
            pltpu.make_async_copy(leaf_out.at[k], leaf_buf.at[k], in_sem.at[1, k]),
        )
        for k in range(8)
    ]
    for pair in loads:
        for copy in pair:
            copy.start()
    stores = []
    for k in range(8):
        for copy in loads[k]:
            copy.wait()
        values = jnp.concatenate([coef_buf[ch, k] for ch in range(CHUNKS)], 1)
        out_buf[k] = jnp.dot(
            realify(leaf_buf[k], RANK), values, preferred_element_type=F32
        ).astype(BF16)
        stores.append(pltpu.make_async_copy(out_buf.at[k], out.at[k], out_sem.at[k]))
        stores[k].start()
    for copy in stores:
        copy.wait()


def body(sources, leaf_in, own_blocks, cross_blocks, leaf_out):
    sources = sources.reshape(8, 2 * LEAF, COLUMNS)
    own_blocks = own_blocks.reshape(LEVELS, 2, 4, RANK, 2 * RANK)
    cross_blocks = cross_blocks.reshape(LEVELS, 2, 4, RANK, 2 * RANK)
    dma = pltpu.SemaphoreType.DMA

    def coefs(count=CHUNKS):
        return pltpu.VMEM((count, 2, 4, 2 * RANK, WIDTH), BF16)

    def blocks(*lead):
        return pltpu.VMEM(lead + (2, 4, RANK, 2 * RANK), BF16)

    coef = pl.pallas_call(
        butterfly,
        out_shape=jax.ShapeDtypeStruct((CHUNKS, 2, 4, 2 * RANK, WIDTH), BF16),
        in_specs=[pl.BlockSpec(memory_space=pltpu.HBM)] * 4,
        out_specs=pl.BlockSpec(memory_space=pl.ANY),
        scratch_shapes=[
            pltpu.VMEM((8, 2 * LEAF, COLUMNS), BF16),
            pltpu.VMEM((8, RANK, 2 * LEAF), BF16),
            blocks(2, 4), blocks(), blocks(2, 2), blocks(2, 2), blocks(2, 3),
            pltpu.VMEM((LEVELS, 4, 4 * RANK, 4 * RANK), BF16),
            coefs(), coefs(2), coefs(), coefs(), coefs(), coefs(), coefs(), coefs(), coefs(), coefs(), coefs(),
            dma((11,)), dma((1,)), dma((1,)), dma((2, 4)), dma((2, 4)), dma((2, 8)), dma((2, 8)), dma((2, 8)), dma((2, 8)),
            dma((CHUNKS,)), dma((CHUNKS,)), dma((CHUNKS, 4)), dma((CHUNKS, 4)), dma((CHUNKS, 4)), dma((CHUNKS, 4)), dma((CHUNKS, 8)), dma((CHUNKS, 8)),
            dma((CHUNKS, 4)), dma((CHUNKS, 4)), dma((CHUNKS, 8)), dma((CHUNKS, 8)),
        ],
        compiler_params=pltpu.CompilerParams(
            collective_id=0, has_side_effects=True, vmem_limit_bytes=60 * 2**20
        ),
        cost_estimate=pl.CostEstimate(flops=3_500_000_000, bytes_accessed=8_000_000, transcendentals=0),
        name="butterfly",
    )(sources, leaf_in, own_blocks, cross_blocks)
    coef = coef.reshape(CHUNKS, 8, 2 * RANK, WIDTH)
    result = pl.pallas_call(
        interpolate,
        out_shape=jax.ShapeDtypeStruct((8, 2 * LEAF, COLUMNS), BF16),
        in_specs=[pl.BlockSpec(memory_space=pltpu.HBM)] * 2,
        out_specs=pl.BlockSpec(memory_space=pltpu.HBM),
        scratch_shapes=[
            pltpu.VMEM((CHUNKS, 8, 2 * RANK, WIDTH), BF16),
            pltpu.VMEM((8, LEAF, 2 * RANK), BF16),
            pltpu.VMEM((8, 2 * LEAF, COLUMNS), BF16),
            dma((2, 8)), dma((8,)),
        ],
        compiler_params=pltpu.CompilerParams(vmem_limit_bytes=60 * 2**20),
        name="interpolate",
    )(coef, leaf_out)
    return result.reshape(8, 2, LEAF, COLUMNS)


def solution(mesh):
    in_specs = (
        P(("grp", "dev"), None, None, None),
        P(("grp", "dev"), None, None),
        P(None, ("grp", "dev"), None, None),
        P(None, ("grp", "dev"), None, None),
        P(("grp", "dev"), None, None),
    )
    out_specs = P(("grp", "dev"), None, None, None)
    return jax.shard_map(body, mesh=mesh, in_specs=in_specs, out_specs=out_specs, check_vma=False)
```

```python
import functools

import jax
import jax.numpy as jnp
from jax import lax
from jax.experimental import pallas as pl
from jax.experimental.pallas import tpu as pltpu
from jax.sharding import PartitionSpec as P

RANK = 64
LEAF = 256
COLUMNS = 512
CHUNKS = 2
WIDTH = COLUMNS // CHUNKS
LEVELS = 11
MESH = pl.DeviceIdType.MESH
F32 = jnp.float32
BF16 = jnp.bfloat16


def div(a, b):
    return a // b if isinstance(a, int) else lax.div(a, jnp.int32(b))


def rem(a, b):
    return a % b if isinstance(a, int) else lax.rem(a, jnp.int32(b))


def xor(a, b, bits):
    total = 0
    for bit in range(bits):
        one, two = rem(div(a, 2**bit), 2), rem(div(b, 2**bit), 2)
        total = total + rem(one + two, 2) * 2**bit
    return total


def device(x, y, z, core):
    return {"grp": div(z, 4) * 4 + x, "dev": rem(z, 4) * 8 + y * 2 + core}


def realify(block, half):
    real_part, imag_part = block[:, :half], block[:, half:]
    upper = jnp.concatenate([real_part, -imag_part], 1)
    lower = jnp.concatenate([imag_part, real_part], 1)
    return jnp.concatenate([upper, lower], 0)


def pairs(bit):
    step = 2**bit
    return [(s, s + step) for s in range(8) if not s & step]


def butterfly(
    sources, leaf_in, own, cross, out,
    src, leaf, w_loc, w_core, w_y, w_z, w_x, big,
    a_buf, b_buf, core_buf, y_send, y_buf, v_send, v_buf, z_buf, x_send, x_buf, r_send,
    load_sem, wc_s, wc_r, wy_s, wy_r, wz_s, wz_r, wx_s, wx_r,
    c_s, c_r, y_s, y_r, v_s, v_r, z_s, z_r, x_s, x_r, r_s, r_r,
):
    grp, dev = lax.axis_index("grp"), lax.axis_index("dev")
    x, y, z = rem(grp, 4), rem(div(dev, 2), 4), div(grp, 4) * 4 + div(dev, 8)
    core = rem(dev, 2)
    z_lo, z_hi = rem(z, 4), div(z, 4)
    sent = []

    def send(from_ref, to_ref, send_sem, recv_sem, target, here=None):
        copy = pltpu.make_async_remote_copy(
            src_ref=from_ref, dst_ref=to_ref, send_sem=send_sem, recv_sem=recv_sem,
            device_id=target, device_id_type=MESH,
        )
        if here is None:
            copy.start()
        else:
            pl.when(here)(pltpu.make_async_copy(from_ref, to_ref, recv_sem).start)
            pl.when(jnp.logical_not(here))(copy.start)
        sent.append((copy, here))

    def keep(from_ref, to_ref, sem):
        pltpu.make_async_copy(from_ref, to_ref, sem).start()

    def arrived(ref, sem):
        pltpu.make_async_copy(ref, ref, sem).wait()

    kinds = (own, cross)
    loads = [pltpu.make_async_copy(leaf_in, leaf, load_sem.at[0])]
    for kind in range(2):
        loads.append(pltpu.make_async_copy(kinds[kind].at[pl.ds(0, 4)], w_loc.at[kind], load_sem.at[1 + kind]))
    for k in range(8):
        loads.append(pltpu.make_async_copy(sources.at[k], src.at[k], load_sem.at[3 + k]))
    for copy in loads:
        copy.start()

    barrier = pltpu.get_barrier_semaphore()

    def greet(target, here=None):
        def signal():
            pl.semaphore_signal(barrier, inc=1, device_id=target, device_id_type=MESH)

        if here is None:
            signal()
        else:
            pl.when(jnp.logical_not(here))(signal)

    greet(device(x, y, z, 1 - core))
    for i in range(1, 4):
        greet(device(x, xor(y, i, 2), z, core))
        greet(device(xor(x, i, 2), y, z, core))
    for m in range(1, 8):
        greet(device(x, y, xor(z, m, 3), core))
    for m in range(8):
        here = None if m else x == 0
        offset = x + 4 * (m // 4)
        greet(device(xor(x, m % 4, 2), y, xor(z, offset, 3), core), here)
        from_x = xor(x, m % 4, 2)
        greet(device(from_x, y, xor(z_lo, from_x, 2) + 4 * xor(z_hi, m // 4, 1), core), here)
    count = 1 + 6 + 7 + 16 - jnp.where(x == 0, 2, 0)

    pl.semaphore_wait(barrier, count)

    for m in range(8):
        q = xor(z, m, 3)
        slot, c = rem(q, 4), div(q, 4)
        for kind in range(2):
            refs = (kinds[kind].at[pl.ds(6, 2), c, slot], w_z.at[kind, :, z_hi, z_lo])
            if m:
                send(*refs, wz_s.at[kind, m], wz_r.at[kind, z], device(x, y, q, core))
            else:
                keep(*refs, wz_r.at[kind, z])
    for m in range(8):
        q = xor(z, m, 3)
        slot, c = rem(q, 4), div(q, 4)
        for kind in range(2):
            send(
                kinds[kind].at[pl.ds(8, 3), c, slot], w_x.at[kind, :, z_hi, x],
                wx_s.at[kind, m], wx_r.at[kind, x + 4 * z_hi],
                device(m % 4, y, q, core), None if m else x == 0,
            )
    send(cross.at[3], w_core, wc_s.at[0], wc_r.at[0], device(x, y, z, 1 - core))
    for i in range(4):
        t = xor(y, i, 2)
        for kind in range(2):
            refs = (kinds[kind].at[pl.ds(4, 2), :, t], w_y.at[kind, :, :, y])
            if i:
                send(*refs, wy_s.at[kind, i], wy_r.at[kind, y], device(x, t, z, core))
            else:
                keep(*refs, wy_r.at[kind, y])

    def assemble(level, bit, w, at, p_range=range(4)):
        for p in p_range:
            s, t = pairs(bit)[p]
            def block(kind, k):
                return realify(w[kind, at, k // 4, k % 4], RANK)
            big[level, p] = jnp.concatenate(
                [
                    jnp.concatenate([block(0, s), block(1, t)], 1),
                    jnp.concatenate([block(1, s), block(0, t)], 1),
                ],
                0,
            )

    loads[1].wait()
    loads[2].wait()
    for level in range(3):
        assemble(level, level, w_loc, level)

    def step(level, bit, source, target, ch_s, ch_t):
        for p, (s, t) in enumerate(pairs(bit)):
            stacked = jnp.concatenate([source[ch_s, s // 4, s % 4], source[ch_s, t // 4, t % 4]], 0)
            value = jnp.dot(big[level, p], stacked, preferred_element_type=F32).astype(BF16)
            target[ch_t, s // 4, s % 4] = value[:128]
            target[ch_t, t // 4, t % 4] = value[128:]

    def levels_local(ch):
        if ch == 0:
            loads[0].wait()
        for k in range(8):
            if ch == 0:
                loads[3 + k].wait()
            a_buf[ch, k // 4, k % 4] = jnp.dot(
                realify(leaf[k], LEAF), src[k, :, ch * WIDTH : (ch + 1) * WIDTH], preferred_element_type=F32
            ).astype(BF16)
        step(0, 0, a_buf, b_buf, ch, 0)
        step(1, 1, b_buf, b_buf, 0, 1)
        step(2, 2, b_buf, a_buf, 1, ch)
        send(a_buf.at[ch], core_buf.at[ch], c_s.at[ch], c_r.at[ch], device(x, y, z, 1 - core))

    def along_y(from_ref, to_ref, ch, send_sem, recv_sem):
        for i in (1, 2, 3, 0):
            t = xor(y, i, 2)
            refs = (from_ref.at[ch, :, t], to_ref.at[ch, :, y])
            if i:
                send(*refs, send_sem.at[ch, i], recv_sem.at[ch, y], device(x, t, z, core))
            else:
                keep(*refs, recv_sem.at[ch, y])

    def level_core(ch):
        if ch == 0:
            arrived(w_core, wc_r.at[0])
            for k in range(8):
                big[3, k // 2, pl.ds(128 * (k % 2), 128)] = jnp.concatenate(
                    [realify(w_loc[0, 3, k // 4, k % 4], RANK), realify(w_core[k // 4, k % 4], RANK)], 1
                )
        arrived(core_buf.at[ch], c_r.at[ch])
        for k in range(8):
            stacked = jnp.concatenate([a_buf[ch, k // 4, k % 4], core_buf[ch, k // 4, k % 4]], 0)
            y_send[ch, k // 4, k % 4] = jnp.dot(
                big[3, k // 2, pl.ds(128 * (k % 2), 128)], stacked, preferred_element_type=F32
            ).astype(BF16)
        along_y(y_send, y_buf, ch, y_s, y_r)

    def levels_y(ch):
        if ch == 0:
            for kind in range(2):
                for t in range(4):
                    arrived(w_y.at[kind, :, :, t], wy_r.at[kind, t])
            for level in (4, 5):
                assemble(level, level - 4, w_y, level - 4)
        for t in range(4):
            arrived(y_buf.at[ch, :, t], y_r.at[ch, t])
        step(4, 0, y_buf, b_buf, ch, 0)
        step(5, 1, b_buf, v_send, 0, ch)
        along_y(v_send, v_buf, ch, v_s, v_r)

    def to_z(ch):
        for t in range(4):
            arrived(v_buf.at[ch, :, t], v_r.at[ch, t])
        for m in (4, 3, 5, 2, 6, 1, 7, 0):
            q = xor(z, m, 3)
            refs = (v_buf.at[ch, div(q, 4), rem(q, 4)], z_buf.at[ch, z_hi, z_lo])
            if m:
                send(*refs, z_s.at[ch, m], z_r.at[ch, z], device(x, y, q, core))
            else:
                keep(*refs, z_r.at[ch, z])

    def levels_z(ch):
        if ch == 0:
            for kind in range(2):
                for k in range(8):
                    arrived(w_z.at[kind, :, k // 4, k % 4], wz_r.at[kind, k])
            for level in (6, 7):
                assemble(level, level - 6, w_z, level - 6)
        for k in range(8):
            arrived(z_buf.at[ch, k // 4, k % 4], z_r.at[ch, k])
        step(6, 0, z_buf, b_buf, ch, 0)
        step(7, 1, b_buf, x_send, 0, ch)
        for i in (1, 2, 3, 0):
            t = xor(x, i, 2)
            refs = (x_send.at[ch, :, xor(t, z_lo, 2)], x_buf.at[ch, :, x])
            if i:
                send(*refs, x_s.at[ch, i], x_r.at[ch, x], device(t, y, z, core))
            else:
                keep(*refs, x_r.at[ch, x])

    def levels_x(ch):
        if ch == 0:
            for kind in range(2):
                for k in range(8):
                    arrived(w_x.at[kind, :, k // 4, k % 4], wx_r.at[kind, k])
            for level in (8, 9, 10):
                assemble(level, level - 8, w_x, level - 8)
        for t in range(4):
            arrived(x_buf.at[ch, :, t], x_r.at[ch, t])
        step(8, 0, x_buf, b_buf, ch, 0)
        step(9, 1, b_buf, b_buf, 0, 1)
        step(10, 2, b_buf, r_send, 1, ch)
        lo = xor(x, z_lo, 2)
        for m in (4, 3, 5, 2, 6, 1, 7, 0):
            t, hi = xor(x, m % 4, 2), xor(z_hi, m // 4, 1)
            send(
                r_send.at[ch, hi, t], out.at[ch, z_hi, z_lo], r_s.at[ch, m], r_r.at[ch, z],
                device(t, y, lo + 4 * hi, core), None if m else x == 0,
            )

    levels_local(0)
    levels_local(1)
    level_core(0)
    levels_y(0)
    level_core(1)
    to_z(0)
    levels_y(1)
    to_z(1)
    for ch in range(CHUNKS):
        levels_z(ch)
        levels_x(ch)
    for ch in range(CHUNKS):
        for k in range(8):
            arrived(out.at[ch, k // 4, k % 4], r_r.at[ch, k])
    for copy, here in sent:
        if here is None:
            copy.wait_send()
        else:
            pl.when(jnp.logical_not(here))(copy.wait_send)


def interpolate(coef, leaf_out, out, coef_buf, leaf_buf, out_buf, in_sem, out_sem):
    loads = [
        (
            pltpu.make_async_copy(coef.at[:, k], coef_buf.at[:, k], in_sem.at[0, k]),
            pltpu.make_async_copy(leaf_out.at[k], leaf_buf.at[k], in_sem.at[1, k]),
        )
        for k in range(8)
    ]
    for pair in loads:
        for copy in pair:
            copy.start()
    stores = []
    for k in range(8):
        for copy in loads[k]:
            copy.wait()
        values = jnp.concatenate([coef_buf[ch, k] for ch in range(CHUNKS)], 1)
        matrix = realify(leaf_buf[k], RANK)
        for part in range(2):
            rows = pl.ds(part * LEAF, LEAF)
            out_buf[k, rows] = jnp.dot(
                matrix[part * LEAF : (part + 1) * LEAF], values, preferred_element_type=F32
            ).astype(BF16)
            stores.append(pltpu.make_async_copy(out_buf.at[k, rows], out.at[k, rows], out_sem.at[part, k]))
            stores[-1].start()
    for copy in stores:
        copy.wait()


def body(sources, leaf_in, own_blocks, cross_blocks, leaf_out):
    sources = sources.reshape(8, 2 * LEAF, COLUMNS)
    own_blocks = own_blocks.reshape(LEVELS, 2, 4, RANK, 2 * RANK)
    cross_blocks = cross_blocks.reshape(LEVELS, 2, 4, RANK, 2 * RANK)
    dma = pltpu.SemaphoreType.DMA

    def coefs(count=CHUNKS):
        return pltpu.VMEM((count, 2, 4, 2 * RANK, WIDTH), BF16)

    def blocks(*lead):
        return pltpu.VMEM(lead + (2, 4, RANK, 2 * RANK), BF16)

    coef = pl.pallas_call(
        butterfly,
        out_shape=jax.ShapeDtypeStruct((CHUNKS, 2, 4, 2 * RANK, WIDTH), BF16),
        in_specs=[pl.BlockSpec(memory_space=pltpu.HBM)] * 4,
        out_specs=pl.BlockSpec(memory_space=pl.ANY),
        scratch_shapes=[
            pltpu.VMEM((8, 2 * LEAF, COLUMNS), BF16),
            pltpu.VMEM((8, RANK, 2 * LEAF), BF16),
            blocks(2, 4), blocks(), blocks(2, 2), blocks(2, 2), blocks(2, 3),
            pltpu.VMEM((LEVELS, 4, 4 * RANK, 4 * RANK), BF16),
            coefs(), coefs(2), coefs(), coefs(), coefs(), coefs(), coefs(), coefs(), coefs(), coefs(), coefs(),
            dma((11,)), dma((1,)), dma((1,)), dma((2, 4)), dma((2, 4)), dma((2, 8)), dma((2, 8)), dma((2, 8)), dma((2, 8)),
            dma((CHUNKS,)), dma((CHUNKS,)), dma((CHUNKS, 4)), dma((CHUNKS, 4)), dma((CHUNKS, 4)), dma((CHUNKS, 4)), dma((CHUNKS, 8)), dma((CHUNKS, 8)),
            dma((CHUNKS, 4)), dma((CHUNKS, 4)), dma((CHUNKS, 8)), dma((CHUNKS, 8)),
        ],
        compiler_params=pltpu.CompilerParams(
            collective_id=0, has_side_effects=True, vmem_limit_bytes=60 * 2**20
        ),
        cost_estimate=pl.CostEstimate(flops=3_500_000_000, bytes_accessed=8_000_000, transcendentals=0),
        name="butterfly",
    )(sources, leaf_in, own_blocks, cross_blocks)
    coef = coef.reshape(CHUNKS, 8, 2 * RANK, WIDTH)
    result = pl.pallas_call(
        interpolate,
        out_shape=jax.ShapeDtypeStruct((8, 2 * LEAF, COLUMNS), BF16),
        in_specs=[pl.BlockSpec(memory_space=pltpu.HBM)] * 2,
        out_specs=pl.BlockSpec(memory_space=pltpu.HBM),
        scratch_shapes=[
            pltpu.VMEM((CHUNKS, 8, 2 * RANK, WIDTH), BF16),
            pltpu.VMEM((8, LEAF, 2 * RANK), BF16),
            pltpu.VMEM((8, 2 * LEAF, COLUMNS), BF16),
            dma((2, 8)), dma((2, 8)),
        ],
        compiler_params=pltpu.CompilerParams(vmem_limit_bytes=60 * 2**20),
        name="interpolate",
    )(coef, leaf_out)
    return result.reshape(8, 2, LEAF, COLUMNS)


def solution(mesh):
    in_specs = (
        P(("grp", "dev"), None, None, None),
        P(("grp", "dev"), None, None),
        P(None, ("grp", "dev"), None, None),
        P(None, ("grp", "dev"), None, None),
        P(("grp", "dev"), None, None),
    )
    out_specs = P(("grp", "dev"), None, None, None)
    return jax.shard_map(body, mesh=mesh, in_specs=in_specs, out_specs=out_specs, check_vma=False)
```
